512 devices in a mesh: partitio: 64 (over z, y), snapshot: 8 (over x, core).
Axes of the slice: x: 4, y: 4, z: 16, core: 2. Of those that a mesh axis runs over, the one named last changes fastest.
Arguments:
- snapshots: float32 [256, 65536], P('snapshot', 'partitio'), may hold values from -50 to 50
- connect: int32 [4, 327680], P(None, 'partitio'), may hold values from 0 to 1023
- elem_mask: int32 [327680], P('partitio'), may hold values from 0 to 1, as said below
- volume: float32 [327680], P('partitio'), may hold values from 0.5 to 4
- owned: int32 [65536], P('partitio'), may hold values 0 or 1
- peer_ids: int32 [64, 4], P('partitio'), may hold values from 0 to 63, as said below
- peer_back: int32 [64, 4], P('partitio'), may hold values from 0 to 3, as said below
- iface_rows: int32 [64, 4, 128], P('partitio'), may hold values from 0 to 1023
- iface_mask: int32 [64, 4, 128], P('partitio'), may hold values from 0 to 1, as said below
Outputs:
- mass_snap: float32 [256, 65536], P('snapshot', 'partitio')
- gram_matrix: float32 [256, 256], P(None, 'partitio')
The draws below stay inside these ranges and needn't reach their ends.
Inputs may be any that keep to these rules, and one draw needn't show every extreme that they name: Each partition's 4 peers are distinct partitions other than itself; q is a peer of p exactly when p is a peer of q, and peer_ids[q, peer_back[p, k]] = p for q = peer_ids[p, k]. `peer_back`: see peer_ids. `iface_mask`: the used slots of each list come first; the list of p for peer q and the list of q for p have the same number of used slots, and slot j of one is the same global node as slot j of the other; at least 32 slots of every list are used and some list uses all 128. `elem_mask`: in each aligned block of 128 element slots the real elements come first, 64 or more of them.
All inputs are finite; a program needn't handle non-finite values. No bound on the sum of `owned` on one device may be relied on, other than what follows from the above.
Results may differ from the reference program's by a relative error of at most 0.000075.
Values sent between devices are 32-bit elements; how exact they have to be, the bound alone decides.
No kernel may reach another device: no remote copies, remote signals or barrier semaphores. Data moves between devices by JAX's collectives and lax.ppermute only.
A program may use at most 64 MiB of HBM per device.

```python
import math
import jax
import jax.numpy as jnp
from jax import lax

SNAP = 256
NODES = 1024
NPEER = 4
SLOT = 128
ELEM = 5120
PARTITIONS = 64


def peer_layout(key):
    base = jax.random.fold_in(key, 11)
    key_order, key_perm, key_count = jax.random.split(base, 3)
    order = jax.random.permutation(key_order, PARTITIONS).astype(jnp.int32)
    position = jnp.argsort(order).astype(jnp.int32)
    scores = jax.random.randint(key_perm, (PARTITIONS, NPEER), 0, 1 << 20) * NPEER + jnp.arange(NPEER, dtype=jnp.int32)[None, :]
    slot_offset = jnp.argsort(scores, axis=1).astype(jnp.int32)
    inverse = jnp.argsort(slot_offset, axis=1).astype(jnp.int32)
    magnitude = slot_offset // 2 + 1
    sign_value = 1 - 2 * (slot_offset % 2)
    own_pos = position[:, None]
    peer_pos = (own_pos + magnitude * sign_value) % PARTITIONS
    peer_list = order[peer_pos]
    back_list = inverse[peer_list, jnp.bitwise_xor(slot_offset, 1)]
    count_table = jax.random.randint(key_count, (PARTITIONS, NPEER // 2), SLOT // 4, SLOT + 1)
    count_table = count_table.at[0, 0].set(SLOT)
    lower_pos = jnp.where(sign_value > 0, own_pos, peer_pos)
    counts = count_table[lower_pos, magnitude - 1]
    live_slots = (jnp.arange(SLOT, dtype=jnp.int32)[None, None, :] < counts[:, :, None]).astype(jnp.int32)
    return (peer_list.astype(jnp.int32), back_list.astype(jnp.int32), live_slots)


def draw_peer_ids(key, part):
    return peer_layout(key)[0]


def draw_peer_back(key, part):
    return peer_layout(key)[1]


def draw_iface_mask(key, part):
    return peer_layout(key)[2]


def draw_elem_mask(key, part):
    counts = jax.random.randint(jax.random.fold_in(key, 3), (PARTITIONS * ELEM // 128, 1), 64, 129)
    live_elems = jnp.arange(128, dtype=jnp.int32)[None, :] < counts
    return live_elems.astype(jnp.int32).reshape(-1)


def draw_snapshots(key, part):
    key_node, key_snap, key_mix, key_mode = jax.random.split(jax.random.fold_in(key, 5), 4)
    total_nodes = PARTITIONS * NODES
    node_scale = jnp.exp(jax.random.uniform(key_node, (1, total_nodes), jnp.float32, math.log(0.3), math.log(3.0)))
    snap_scale = jnp.exp(jax.random.uniform(key_snap, (SNAP, 1), jnp.float32, math.log(0.3), math.log(3.0)))
    column = jnp.arange(SNAP, dtype=jnp.int32) + 1
    levels = jnp.arange(1, 17, dtype=jnp.int32)
    inside = (levels[None, :] * levels[None, :] * column[:, None] <= 256).astype(jnp.int32)
    bound = jnp.maximum(1, jnp.sum(inside, axis=1))
    raw_mix = jax.random.randint(key_mix, (SNAP, SNAP), 0, 1 << 20)
    mixing = (raw_mix % (2 * bound[None, :] + 1) - bound[None, :]).astype(jnp.float32)
    mix_var = jnp.sum(bound * (bound + 1)).astype(jnp.float32) / 3.0
    modes = jax.random.randint(key_mode, (SNAP, total_nodes), -6, 7).astype(jnp.float32)
    mode_var = 14.0
    mixed = jnp.dot(mixing, modes, precision=lax.Precision.HIGHEST, preferred_element_type=jnp.float32)
    field_values = mixed / jnp.sqrt(mix_var * mode_var)
    field_values = jnp.clip(field_values, -5.5, 5.5)
    return (node_scale * snap_scale * field_values).astype(jnp.float32)


def set_ends(drawn, stream_key, low, top_value):
    longest = drawn.shape.index(max(drawn.shape))
    spots = []
    for shift in (0, 1):
        where = [jax.random.randint(jax.random.fold_in(stream_key, axis), (), 0, length) for axis, length in enumerate(drawn.shape)]
        where[longest] = (where[longest] + shift) % drawn.shape[longest]
        spots.append(tuple(where))
    return drawn.at[spots[0]].set(low).at[spots[1]].set(top_value)


def shard_levels(key, dims, cuts, least, top_value):
    def one(axis_at, parts):
        steps = jax.random.uniform(jax.random.fold_in(jax.random.fold_in(key, 6), axis_at), (parts,), jnp.float32, least / len(cuts), top_value / len(cuts))
        return jnp.repeat(jnp.exp(steps), dims[axis_at] // parts).reshape((-1,) + (1,) * (len(dims) - axis_at - 1))

    gain = one(*cuts[0])
    for cut in cuts[1:]:
        gain = gain * one(*cut)
    return gain


def setup_inputs(seed: int = 0) -> dict:
    keys = jax.random.split(jax.random.key(seed), 10)
    snapshots = draw_snapshots(jax.random.fold_in(keys[9], 71), 0)
    connect = set_ends(jax.random.randint(keys[1], (4, PARTITIONS * ELEM), 0, NODES), jax.random.fold_in(keys[1], 1), 0, NODES - 1).astype(jnp.int32)
    elem_mask = draw_elem_mask(jax.random.fold_in(keys[9], 71), 0)
    volume = jnp.clip(jnp.exp(math.log(4.0) - 2.0794415 * jax.random.uniform(keys[3], (PARTITIONS * ELEM,), jnp.float32) ** shard_levels(keys[3], (PARTITIONS * ELEM,), ((0, 64),), -0.2, 0.2)), 0.5, 4.0)
    owned = set_ends((jax.random.randint(keys[4], (PARTITIONS * NODES,), 0, 4) < 3).astype(jnp.int32), jax.random.fold_in(keys[4], 1), 0, 1)
    peer_ids = draw_peer_ids(jax.random.fold_in(keys[9], 71), 0)
    peer_back = draw_peer_back(jax.random.fold_in(keys[9], 71), 0)
    iface_rows = set_ends(jax.random.randint(keys[7], (PARTITIONS, NPEER, SLOT), 0, NODES), jax.random.fold_in(keys[7], 1), 0, NODES - 1).astype(jnp.int32)
    iface_mask = draw_iface_mask(jax.random.fold_in(keys[9], 71), 0)
    return {"snapshots": snapshots, "connect": connect, "elem_mask": elem_mask, "volume": volume, "owned": owned, "peer_ids": peer_ids, "peer_back": peer_back, "iface_rows": iface_rows, "iface_mask": iface_mask}


def local_mass(snap_part, conn_part, weight_part):
    values = snap_part[:, conn_part]
    elem_sum = jnp.sum(values, axis=1, keepdims=True)
    contrib = (values + elem_sum) * weight_part[None, None, :]
    flat_rows = contrib.reshape(snap_part.shape[0], -1)
    return jnp.zeros_like(snap_part).at[:, conn_part.reshape(-1)].add(flat_rows)


def reference(snapshots, connect, elem_mask, volume, owned, peer_ids, peer_back, iface_rows, iface_mask):
    by_part = snapshots.reshape(SNAP, PARTITIONS, NODES).transpose(1, 0, 2)
    conn_parts = connect.reshape(4, PARTITIONS, ELEM).transpose(1, 0, 2)
    weights = (volume * (elem_mask.astype(jnp.float32) * 0.05)).reshape(PARTITIONS, ELEM)

    def one_part(item_set):
        return local_mass(item_set[0], item_set[1], item_set[2])

    local_all = lax.map(one_part, (by_part, conn_parts, weights))

    def assemble(item_set):
        part_index, peer_list, back_list, own_rows, live_slots = item_set
        source_rows = iface_rows[peer_list, back_list]

        def fetch(peer_index, row_list):
            return jnp.take(local_all[peer_index], row_list, axis=1)

        fetched = jax.vmap(fetch)(peer_list, source_rows)
        fetched = fetched * live_slots.astype(jnp.float32)[:, None, :]
        flat_rows = fetched.transpose(1, 0, 2).reshape(SNAP, -1)
        return local_all[part_index].at[:, own_rows.reshape(-1)].add(flat_rows)

    part_list = jnp.arange(PARTITIONS, dtype=jnp.int32)
    assembled = lax.map(assemble, (part_list, peer_ids, peer_back, iface_rows, iface_mask))
    mass_snap = assembled.transpose(1, 0, 2).reshape(SNAP, PARTITIONS * NODES)
    owned_snap = snapshots * owned.astype(jnp.float32)[None, :]
    gram_matrix = lax.dot_general(owned_snap, mass_snap, (((1,), (1,)), ((), ())),
                                  precision=lax.Precision.HIGHEST,
                                  preferred_element_type=jnp.float32) / (PARTITIONS * NODES)
    return mass_snap, gram_matrix
```

```python
import jax
import jax.numpy as jnp
from jax import lax
from jax.experimental import pallas as pl
from jax.experimental.pallas import tpu as pltpu
from jax.sharding import Mesh, PartitionSpec as P

F32 = jnp.float32
BF16 = jnp.bfloat16
NT = (((1,), (1,)), ((), ()))
CHUNK = 512
LANES = 128


def split2(x):
    high = x.astype(BF16)
    low = (x - high.astype(F32)).astype(BF16)
    return jnp.concatenate([high, low], axis=0)


def one_hot_block(lists, first, rows):
    iota = lax.broadcasted_iota(jnp.int32, (rows, lists[0].shape[1]), 0).astype(F32).astype(BF16)
    count = None
    for entry in lists:
        near = (entry - first).astype(F32).astype(BF16)
        hit = jnp.where(iota == near, jnp.ones((), BF16), jnp.zeros((), BF16))
        count = hit if count is None else count + hit
    return count


def fill_one_hot(ref, lists):
    for first in range(0, ref.shape[0], 256):
        ref[first : first + 256, :] = one_hot_block(lists, first, 256)


def local_kernel(peer_ref, snap_ref, conn_ref, mask_ref, vol_ref, rows_ref, mass_ref, send_ref, hot_ref, acc_ref, slot_ref):
    snaps = snap_ref.shape[0]
    snap = snap_ref[...]
    snap2 = split2(snap)
    acc_ref[...] = jnp.zeros_like(acc_ref)
    for step in range(conn_ref.shape[1] // CHUNK):
        cols = slice(step * CHUNK, (step + 1) * CHUNK)
        hot = hot_ref.at[step % 2]
        fill_one_hot(hot, [conn_ref[i : i + 1, cols] for i in range(4)])
        weight = vol_ref[:, cols] * (mask_ref[:, cols].astype(F32) * 0.05)
        both = jnp.dot(snap2, hot[...], preferred_element_type=F32)
        value = (both[:snaps] + both[snaps:]) * weight
        weight2 = split2(jnp.broadcast_to(weight, (8, CHUNK)))
        left = jnp.concatenate([split2(value), weight2], axis=0)
        acc_ref[...] += lax.dot_general(left, hot[...], NT, preferred_element_type=F32)
    diag = acc_ref[2 * snaps : 2 * snaps + 1] + acc_ref[2 * snaps + 8 : 2 * snaps + 9]
    mass = acc_ref[:snaps] + acc_ref[snaps : 2 * snaps] + snap * diag
    mass_ref[...] = mass
    fill_one_hot(slot_ref, [jnp.concatenate([rows_ref[k : k + 1, :] for k in range(4)], axis=1)])
    both = jnp.dot(split2(mass), slot_ref[...], preferred_element_type=F32)
    picked = both[:snaps] + both[snaps:]
    send_ref[...] = jnp.zeros_like(send_ref)
    for k in range(4):
        send_ref[peer_ref[0, k]] = picked[:, k * LANES : (k + 1) * LANES]


def final_kernel(peer_ref, recv_ref, rows_ref, live_ref, mass_ref, all_ref, owned_ref, out_ref, gram_ref, slot_ref):
    snaps = mass_ref.shape[0]
    parts = []
    for k in range(4):
        live = live_ref[k : k + 1, :].astype(F32)
        parts.append(recv_ref[peer_ref[0, k]] * live)
    fill_one_hot(slot_ref, [jnp.concatenate([rows_ref[k : k + 1, :] for k in range(4)], axis=1)])
    added = lax.dot_general(split2(jnp.concatenate(parts, axis=1)), slot_ref[...], NT, preferred_element_type=F32)
    total = mass_ref[...] + (added[:snaps] + added[snaps:])
    out_ref[...] = total
    left = split2(all_ref[...] * owned_ref[...].astype(F32))
    both = lax.dot_general(split2(total), left, NT, preferred_element_type=F32)
    count = all_ref.shape[0]
    gram_ref[...] = (
        both[:snaps, :count] + (both[snaps:, :count] + both[:snaps, count:])
    )


def vmem(count):
    return [pl.BlockSpec(memory_space=pltpu.VMEM)] * count


def per_device(snapshots, connect, elem_mask, volume, owned, peer_ids, peer_back, iface_rows, iface_mask):
    snaps, nodes = snapshots.shape
    zs, ys = lax.axis_size("z"), lax.axis_size("y")
    groups = lax.axis_size("x") * lax.axis_size("core")
    parts = zs * ys
    params = pltpu.CompilerParams(vmem_limit_bytes=40 * 1024 * 1024)
    smem = pl.BlockSpec(memory_space=pltpu.SMEM)
    all_snaps = lax.all_gather(snapshots, ("x", "core"), axis=0, tiled=True)
    mass, send = pl.pallas_call(
        local_kernel,
        out_shape=(
            jax.ShapeDtypeStruct((snaps, nodes), F32),
            jax.ShapeDtypeStruct((parts, snaps, LANES), F32),
        ),
        in_specs=[smem] + vmem(5),
        out_specs=tuple(vmem(2)),
        scratch_shapes=[
            pltpu.VMEM((2, nodes, CHUNK), BF16),
            pltpu.VMEM((2 * snaps + 16, nodes), F32),
            pltpu.VMEM((nodes, 4 * LANES), BF16),
        ],
        compiler_params=params,
        name="local_mass",
    )(peer_ids, snapshots, connect, elem_mask[None], volume[None], iface_rows[0])
    recv = lax.all_to_all(send, ("z", "y"), 0, 0, tiled=True)
    mass_snap, gram = pl.pallas_call(
        final_kernel,
        out_shape=(
            jax.ShapeDtypeStruct((snaps, nodes), F32),
            jax.ShapeDtypeStruct((snaps, snaps * groups), F32),
        ),
        in_specs=[smem] + vmem(6),
        out_specs=tuple(vmem(2)),
        scratch_shapes=[pltpu.VMEM((nodes, 4 * LANES), BF16)],
        compiler_params=params,
        name="assemble_gram",
    )(peer_ids, recv, iface_rows[0], iface_mask[0], mass, all_snaps, owned[None])
    gram = gram * (1.0 / (parts * nodes))
    per_z = snaps // (ys * 4)
    gram = gram.reshape(per_z, ys, 4, groups, snaps).transpose(1, 3, 0, 2, 4)
    gram = lax.all_to_all(gram.reshape(ys * groups, per_z * 4 * snaps), ("y", "x", "core"), 0, 0, tiled=True)
    gram = jnp.sum(gram.reshape(ys, zs, 4 * snaps), axis=0)
    gram = lax.all_to_all(gram, "z", 0, 0, tiled=True)
    gram = jnp.sum(gram.reshape(zs, 1, 4 * snaps), axis=0)
    gram = lax.all_to_all(jnp.broadcast_to(gram, (groups, 4 * snaps)), ("x", "core"), 0, 0, tiled=True)
    gram = gram.reshape(groups, 4, snaps).transpose(0, 2, 1).reshape(groups * snaps, 4)
    return mass_snap, gram


def solution(mesh):
    sizes = (16, 4, 4, 2)
    fine = Mesh(mesh.devices.reshape(sizes), ("z", "y", "x", "core"))
    part, snap = ("z", "y"), ("x", "core")
    in_specs = (
        P(snap, part),
        P(None, part),
        P(part),
        P(part),
        P(part),
        P(part, None),
        P(part, None),
        P(part, None, None),
        P(part, None, None),
    )
    out_specs = (P(snap, part), P(None, part))
    return jax.shard_map(per_device, mesh=fine, in_specs=in_specs, out_specs=out_specs, check_vma=False)
```

```python
import jax
import jax.numpy as jnp
from jax import lax
from jax.experimental import pallas as pl
from jax.experimental.pallas import tpu as pltpu
from jax.sharding import Mesh, PartitionSpec as P

F32 = jnp.float32
BF16 = jnp.bfloat16
NT = (((1,), (1,)), ((), ()))
CHUNK = 512
LANES = 128
SLOTS = 4
OVERFLOW = 1e30


def split2(x):
    high = x.astype(BF16)
    low = (x - high.astype(F32)).astype(BF16)
    return jnp.concatenate([high, low], axis=0)


def one_hot_block(lists, first, rows):
    iota = lax.broadcasted_iota(jnp.int32, (rows, lists[0].shape[1]), 0).astype(F32).astype(BF16)
    count = None
    for entry in lists:
        near = (entry - first).astype(F32).astype(BF16)
        hit = jnp.where(iota == near, jnp.ones((), BF16), jnp.zeros((), BF16))
        count = hit if count is None else count + hit
    return count


def fill_one_hot(ref, lists):
    for first in range(0, ref.shape[0], 256):
        ref[first : first + 256, :] = one_hot_block(lists, first, 256)


def local_kernel(snap_ref, conn_ref, mask_ref, vol_ref, mass_ref, hot_ref, acc_ref):
    snaps = snap_ref.shape[0]
    snap = snap_ref[...]
    snap2 = split2(snap)
    acc_ref[...] = jnp.zeros_like(acc_ref)
    for step in range(conn_ref.shape[1] // CHUNK):
        cols = slice(step * CHUNK, (step + 1) * CHUNK)
        hot = hot_ref.at[step % 2]
        fill_one_hot(hot, [conn_ref[i : i + 1, cols] for i in range(4)])
        weight = vol_ref[:, cols] * (mask_ref[:, cols].astype(F32) * 0.05)
        both = jnp.dot(snap2, hot[...], preferred_element_type=F32)
        value = (both[:snaps] + both[snaps:]) * weight
        weight2 = split2(jnp.broadcast_to(weight, (8, CHUNK)))
        left = jnp.concatenate([split2(value), weight2], axis=0)
        acc_ref[...] += lax.dot_general(left, hot[...], NT, preferred_element_type=F32)
    diag = acc_ref[2 * snaps : 2 * snaps + 1] + acc_ref[2 * snaps + 8 : 2 * snaps + 9]
    mass = acc_ref[:snaps] + acc_ref[snaps : 2 * snaps] + snap * diag
    mass_ref[...] = mass


def pick_kernel(peer_ref, back_ref, mass_ref, rows_ref, _, send_ref, slot_ref):
    mass = mass_ref[...]
    snaps = mass.shape[0]
    fill_one_hot(slot_ref, [jnp.concatenate([rows_ref[k : k + 1, :] for k in range(4)], axis=1)])
    both = jnp.dot(split2(mass), slot_ref[...], preferred_element_type=F32)
    picked = both[:snaps] + both[snaps:]
    for carrier in range(4):
        for k in range(4):
            send_ref[carrier, k] = picked[carrier * 8 : carrier * 8 + 8, k * LANES : (k + 1) * LANES]
            send_ref[carrier, 4, k : k + 1] = jnp.full((1, LANES), peer_ref[0, k], jnp.int32).astype(F32)
            send_ref[carrier, 4, 4 + k : 5 + k] = jnp.full((1, LANES), back_ref[0, k], jnp.int32).astype(F32)


def to_row(column, inside):
    return jnp.sum(jnp.where(inside, column, 0), axis=0, keepdims=True)


def spread_kernel(slots, recv_ref, send_ref, table_ref, place_ref, dma_sem):
    me = lax.axis_index("z")
    ids = jnp.concatenate([recv_ref[y, 4, 0:4] for y in range(4)], axis=0).astype(jnp.int32)
    backs = jnp.concatenate([recv_ref[y, 4, 4:8] for y in range(4)], axis=0).astype(jnp.int32)
    lane = lax.broadcasted_iota(jnp.int32, (16, LANES), 1)
    sub = lax.broadcasted_iota(jnp.int32, (16, LANES), 0)
    line = ids // 4
    key = (ids % 4) * 4 + backs
    same = (line == to_row(line, lane == sub)) & (lane < 16)
    sent = jnp.sum(jnp.where(same & (lane < sub), 1, 0), axis=1, keepdims=True)
    came = jnp.sum(jnp.where(same & (to_row(key, lane == sub) < key), 1, 0), axis=1, keepdims=True)
    home = line == me
    target = line * slots + jnp.where(home, 0, jnp.minimum(sent, slots - 1))
    source = jnp.where(
        home, zs_of(send_ref, slots) * slots + (ids % 4) * 5 + backs, line * slots + jnp.minimum(came, slots - 1)
    )
    table_ref[...] = jnp.where(lane == 0, target, source)
    copy = pltpu.make_async_copy(table_ref, place_ref, dma_sem)
    copy.start()
    send_ref[...] = jnp.zeros_like(send_ref)
    over = jnp.max(jnp.where(home, 0, sent - (slots - 1)), axis=0, keepdims=True) > 0
    copy.wait()
    for y in range(4):
        for k in range(4):
            send_ref[place_ref[y * 4 + k, 0]] = recv_ref[y, k]
    for z in range(zs_of(send_ref, slots)):
        send_ref[z * slots] = jnp.where(over, OVERFLOW, send_ref[z * slots])


def zs_of(ref, slots):
    return ref.shape[0] // slots


def collect_kernel(slots, table_ref, near_ref, far_ref, send_ref, flag_ref, place_ref, dma_sem):
    copy = pltpu.make_async_copy(table_ref, place_ref, dma_sem)
    copy.start()
    top = far_ref[0]
    for z in range(1, zs_of(far_ref, slots)):
        top = jnp.maximum(top, far_ref[z * slots])
    flag_ref[0, 0] = (jnp.max(top) > OVERFLOW * 0.5).astype(jnp.int32)
    copy.wait()
    total = far_ref.shape[0]
    for y in range(4):
        for k in range(4):
            place = place_ref[y * 4 + k, 1]
            far = far_ref[jnp.minimum(place, total - 1)]
            near = near_ref[jnp.maximum(place - total, 0)]
            send_ref[y, k] = jnp.where(place < total, far, near)


def final_kernel(recv_ref, rows_ref, live_ref, mass_ref, same_ref, other_ref, owned_ref, out_ref, gram_ref, slot_ref):
    snaps = mass_ref.shape[0]
    parts = []
    for k in range(4):
        live = live_ref[k : k + 1, :].astype(F32)
        parts.append(jnp.concatenate([recv_ref[y, k] for y in range(4)], axis=0) * live)
    fill_one_hot(slot_ref, [jnp.concatenate([rows_ref[k : k + 1, :] for k in range(4)], axis=1)])
    added = lax.dot_general(split2(jnp.concatenate(parts, axis=1)), slot_ref[...], NT, preferred_element_type=F32)
    total = mass_ref[...] + (added[:snaps] + added[snaps:])
    out_ref[...] = total
    total2 = split2(total)
    owned = owned_ref[...].astype(F32)
    core = lax.axis_index("core")
    for index, ref in ((core, same_ref), (1 - core, other_ref)):
        count = ref.shape[0]
        both = lax.dot_general(total2, split2(ref[...] * owned), NT, preferred_element_type=F32)
        gram_ref[index] = both[:snaps, :count] + (both[snaps:, :count] + both[:snaps, count:])


def gather_kernel(scale, recv_ref, out_ref):
    total = recv_ref[0]
    for z in range(1, recv_ref.shape[0]):
        total = total + recv_ref[z]
    total = total * scale
    groups, columns = total.shape[0], out_ref.shape[0]
    width = LANES // columns
    for c in range(columns):
        for half in range(groups // columns):
            out_ref[c : c + 1, half * LANES : (half + 1) * LANES] = jnp.concatenate(
                [total[half * columns + q : half * columns + q + 1, c * width : (c + 1) * width] for q in range(columns)],
                axis=1,
            )


def vmem(count):
    return [pl.BlockSpec(memory_space=pltpu.VMEM)] * count


SMEM = pl.BlockSpec(memory_space=pltpu.SMEM)
HBM = pl.BlockSpec(memory_space=pltpu.HBM)
ANY = pl.BlockSpec(memory_space=pl.ANY)


def route(recv, slots, zs):
    scratch = [pltpu.SMEM((16, LANES), jnp.int32), pltpu.SemaphoreType.DMA]
    send, table = pl.pallas_call(
        lambda *refs: spread_kernel(slots, *refs),
        out_shape=(jax.ShapeDtypeStruct((zs * slots, 8, LANES), F32), jax.ShapeDtypeStruct((16, LANES), jnp.int32)),
        in_specs=vmem(1),
        out_specs=tuple(vmem(2)),
        scratch_shapes=scratch,
        name="spread",
    )(recv)
    far = lax.all_to_all(send, "z", 0, 0, tiled=True)
    return pl.pallas_call(
        lambda *refs: collect_kernel(slots, *refs),
        out_shape=(jax.ShapeDtypeStruct((4, 4, 8, LANES), F32), jax.ShapeDtypeStruct((1, 1), jnp.int32)),
        in_specs=vmem(3),
        out_specs=(vmem(1)[0], SMEM),
        scratch_shapes=scratch,
        name="collect",
    )(table, recv.reshape(20, 8, LANES), far)


def per_device(snapshots, connect, elem_mask, volume, owned, peer_ids, peer_back, iface_rows, iface_mask):
    snaps, nodes = snapshots.shape
    zs, ys = lax.axis_size("z"), lax.axis_size("y")
    groups = lax.axis_size("x") * lax.axis_size("core")
    params = pltpu.CompilerParams(vmem_limit_bytes=40 * 1024 * 1024)
    xs, cores = lax.axis_size("x"), lax.axis_size("core")
    snaps_x = lax.all_to_all(jnp.broadcast_to(snapshots, (xs, snaps, nodes)), "x", 0, 0, tiled=True)
    snaps_x = snaps_x.reshape(xs * snaps, nodes)
    snaps_other = lax.ppermute(snaps_x, "core", [(c, (c + 1) % cores) for c in range(cores)])
    mass = pl.pallas_call(
        local_kernel,
        out_shape=jax.ShapeDtypeStruct((snaps, nodes), F32),
        in_specs=vmem(4),
        out_specs=vmem(1)[0],
        scratch_shapes=[pltpu.VMEM((2, nodes, CHUNK), BF16), pltpu.VMEM((2 * snaps + 16, nodes), F32)],
        compiler_params=params,
        cost_estimate=pl.CostEstimate(flops=10**10, bytes_accessed=10**6, transcendentals=0),
        name="local_mass",
    )(snapshots, connect, elem_mask[None], volume[None])
    send = pl.pallas_call(
        pick_kernel,
        out_shape=jax.ShapeDtypeStruct((ys, 5, 8, LANES), F32),
        in_specs=[SMEM, SMEM] + vmem(2) + [ANY],
        out_specs=vmem(1)[0],
        scratch_shapes=[pltpu.VMEM((nodes, 4 * LANES), BF16)],
        compiler_params=params,
        name="pick",
    )(peer_ids, peer_back, mass, iface_rows[0], snaps_x)
    recv = lax.all_to_all(send, "y", 0, 0, tiled=True)
    picked, short = route(recv, SLOTS, zs)
    picked = lax.cond(short[0, 0] > 0, lambda r, p: route(r, 16, zs)[0], lambda r, p: p, recv, picked)
    recv = lax.all_to_all(picked, "y", 0, 0, tiled=True)
    mass_snap, gram = pl.pallas_call(
        final_kernel,
        out_shape=(
            jax.ShapeDtypeStruct((snaps, nodes), F32),
            jax.ShapeDtypeStruct((cores, snaps, xs * snaps), F32),
        ),
        in_specs=vmem(7),
        out_specs=tuple(vmem(2)),
        scratch_shapes=[pltpu.VMEM((nodes, 4 * LANES), BF16)],
        compiler_params=params,
        name="assemble_gram",
    )(recv, iface_rows[0], iface_mask[0], mass, snaps_x, snaps_other, owned[None])
    per_z = snaps // (ys * 4)
    gram = gram.reshape(cores, per_z, ys, 4, xs, snaps).transpose(2, 4, 0, 1, 3, 5)
    gram = lax.all_to_all(gram.reshape(ys * groups, per_z * 4 * snaps), ("y", "x", "core"), 0, 0, tiled=True)
    gram = jnp.sum(gram.reshape(ys, zs, 1, 4 * snaps), axis=0)
    gram = jnp.broadcast_to(gram, (zs, groups, 4 * snaps)).reshape(zs * groups, 4 * snaps)
    gram = lax.all_to_all(gram, ("z", "x", "core"), 0, 0, tiled=True)
    gram = pl.pallas_call(
        lambda *refs: gather_kernel(1.0 / (zs * ys * nodes), *refs),
        out_shape=jax.ShapeDtypeStruct((4, groups * snaps), F32),
        in_specs=vmem(1),
        out_specs=vmem(1)[0],
        name="sum_columns",
    )(gram.reshape(zs, groups, 4 * snaps))
    return mass_snap, gram.T


def solution(mesh):
    sizes = (16, 4, 4, 2)
    fine = Mesh(mesh.devices.reshape(sizes), ("z", "y", "x", "core"))
    part, snap = ("z", "y"), ("x", "core")
    in_specs = (
        P(snap, part),
        P(None, part),
        P(part),
        P(part),
        P(part),
        P(part, None),
        P(part, None),
        P(part, None, None),
        P(part, None, None),
    )
    out_specs = (P(snap, part), P(None, part))
    return jax.shard_map(per_device, mesh=fine, in_specs=in_specs, out_specs=out_specs, check_vma=False)
```

```python
import jax
import jax.numpy as jnp
from jax import lax
from jax.experimental import pallas as pl
from jax.experimental.pallas import tpu as pltpu
from jax.sharding import Mesh, PartitionSpec as P

F32 = jnp.float32
BF16 = jnp.bfloat16
NT = (((1,), (1,)), ((), ()))
CHUNK = 256
LANES = 128
SLOTS = 4
OVERFLOW = 1e30


def split2(x):
    high = x.astype(BF16)
    low = (x - high.astype(F32)).astype(BF16)
    return jnp.concatenate([high, low], axis=0)


def one_hot_block(lists, first, rows):
    iota = lax.broadcasted_iota(jnp.int32, (rows, lists[0].shape[1]), 0).astype(F32).astype(BF16)
    count = None
    for entry in lists:
        near = (entry - first).astype(F32).astype(BF16)
        hit = jnp.where(iota == near, jnp.ones((), BF16), jnp.zeros((), BF16))
        count = hit if count is None else count + hit
    return count


def fill_one_hot(ref, lists):
    for first in range(0, ref.shape[0], 256):
        ref[first : first + 256, :] = one_hot_block(lists, first, 256)


def local_kernel(peer_ref, back_ref, *refs):
    far, (mass_ref, send_ref), here, (hot_ref, left_ref, acc_ref, slot_ref, sems) = refs[:6], refs[6:8], refs[8:14], refs[14:]
    copies = [pltpu.make_async_copy(a, b, sems.at[i]) for i, (a, b) in enumerate(zip(far, here))]
    for copy in copies:
        copy.start()
    snap_ref, conn_ref, mask_ref, vol_ref, rows_ref, live_ref = here
    for copy in copies:
        copy.wait()
    snaps = snap_ref.shape[0]
    snap = snap_ref[...]
    snap2 = split2(snap)
    steps = conn_ref.shape[1] // CHUNK

    def fill(step):
        cols = slice(step * CHUNK, (step + 1) * CHUNK)
        fill_one_hot(hot_ref.at[step % 2], [conn_ref[i : i + 1, cols] for i in range(4)])

    def element(step):
        cols = slice(step * CHUNK, (step + 1) * CHUNK)
        weight = vol_ref[:, cols] * (mask_ref[:, cols].astype(F32) * 0.05)
        both = jnp.dot(snap2, hot_ref[step % 2], preferred_element_type=F32)
        value = (both[:snaps] + both[snaps:]) * weight
        left_ref[step % 2] = jnp.concatenate([split2(value), split2(jnp.broadcast_to(weight, (8, CHUNK)))], axis=0)

    def add(step):
        part = lax.dot_general(left_ref[step % 2], hot_ref[step % 2], NT, preferred_element_type=F32)
        acc_ref[...] = part if step == 0 else acc_ref[...] + part

    fill(0)
    for step in range(steps):
        element(step)
        if step > 0:
            add(step - 1)
        if step + 1 < steps:
            fill(step + 1)
    add(steps - 1)
    diag = acc_ref[2 * snaps : 2 * snaps + 1] + acc_ref[2 * snaps + 8 : 2 * snaps + 9]
    mass = acc_ref[:snaps] + acc_ref[snaps : 2 * snaps] + snap * diag
    mass_ref[...] = mass
    fill_one_hot(slot_ref, [jnp.concatenate([rows_ref[k : k + 1, :] for k in range(4)], axis=1)])
    both = jnp.dot(split2(mass), slot_ref[...], preferred_element_type=F32)
    picked = both[:snaps] + both[snaps:]
    used = jnp.sum(live_ref[...].astype(F32), axis=1, keepdims=True)
    for carrier in range(4):
        for k in range(4):
            send_ref[carrier, k] = picked[carrier * 8 : carrier * 8 + 8, k * LANES : (k + 1) * LANES]
            whence = jnp.full((1, LANES), peer_ref[0, k] * 4 + back_ref[0, k], jnp.int32)
            send_ref[carrier, 4, k : k + 1] = whence.astype(F32)
        send_ref[carrier, 4, 4:8] = jnp.broadcast_to(used, (4, LANES))


def to_row(column, inside):
    return jnp.sum(jnp.where(inside, column, 0), axis=0, keepdims=True)


def spread_kernel(slots, recv_ref, send_ref, table_ref, place_ref, dma_sem):
    me = lax.axis_index("z")
    whence = jnp.concatenate([recv_ref[y, 4, 0:4] for y in range(4)], axis=0).astype(jnp.int32)
    used = jnp.concatenate([recv_ref[y, 4, 4:8] for y in range(4)], axis=0).astype(jnp.int32)
    lane = lax.broadcasted_iota(jnp.int32, (16, LANES), 1)
    sub = lax.broadcasted_iota(jnp.int32, (16, LANES), 0)
    line = whence // 16
    key = whence % 16
    same = (line == to_row(line, lane == sub)) & (lane < 16)
    width = to_row(used, lane == sub)
    sent = jnp.sum(jnp.where(same & (lane < sub), width, 0), axis=1, keepdims=True)
    came = jnp.sum(jnp.where(same & (to_row(key, lane == sub) < key), width, 0), axis=1, keepdims=True)
    home = line == me
    sent = jnp.where(home, 0, sent)
    total = send_ref.shape[0]
    last = line * slots + slots - 1
    there = line * slots + jnp.minimum(sent // LANES, slots - 1)
    here = line * slots + jnp.minimum(came // LANES, slots - 1)
    near = total + (key // 4) * 5 + key % 4
    table = jnp.where(lane == 0, there, jnp.minimum(there + 1, last))
    table = jnp.where(lane == 2, sent % LANES, table)
    table = jnp.where(lane == 3, jnp.where(home, near, here), table)
    table = jnp.where(lane == 4, jnp.where(home, near, jnp.minimum(here + 1, last)), table)
    table_ref[...] = jnp.where(lane == 5, jnp.where(home, 0, came % LANES), table)
    copy = pltpu.make_async_copy(table_ref, place_ref, dma_sem)
    copy.start()
    send_ref[...] = jnp.zeros_like(send_ref)
    over = jnp.max(jnp.where(home, 0, sent + used - slots * LANES), axis=0, keepdims=True)[:, 0:1] > 0
    tile_lane = lax.broadcasted_iota(jnp.int32, (8, LANES), 1)
    copy.wait()
    for y in range(4):
        for k in range(4):
            e = y * 4 + k
            shift = place_ref[e, 2]
            live = tile_lane < recv_ref[y, 4, 4 + k : 5 + k].astype(jnp.int32)
            moved = pltpu.roll(jnp.where(live, recv_ref[y, k], 0.0), shift, 1)
            first, second = place_ref[e, 0], place_ref[e, 1]
            send_ref[first] = send_ref[first] + jnp.where(tile_lane >= shift, moved, 0.0)
            send_ref[second] = send_ref[second] + jnp.where(tile_lane < shift, moved, 0.0)
    for z in range(zs_of(send_ref, slots)):
        send_ref[z * slots] = jnp.where(over, OVERFLOW, send_ref[z * slots])


def zs_of(ref, slots):
    return ref.shape[0] // slots


def collect_kernel(slots, table_ref, near_ref, far_ref, *refs):
    *blocks, send_ref, flag_ref, all_ref, place_ref, dma_sem = refs
    copy = pltpu.make_async_copy(table_ref, place_ref, dma_sem)
    copy.start()
    top = far_ref[0]
    for z in range(1, zs_of(far_ref, slots)):
        top = jnp.maximum(top, far_ref[z * slots])
    flag_ref[...] = jnp.where(top[0:1, 0:1] > OVERFLOW * 0.5, 1, 0)
    for index, block in enumerate(blocks):
        rows = block.shape[0]
        all_ref[index * rows : (index + 1) * rows] = block[...]
    copy.wait()
    total = far_ref.shape[0]
    tile_lane = lax.broadcasted_iota(jnp.int32, (8, LANES), 1)
    for y in range(4):
        for k in range(4):
            e = y * 4 + k
            first, second, shift = place_ref[e, 3], place_ref[e, 4], place_ref[e, 5]
            begin, rest = far_ref[jnp.minimum(first, total - 1)], far_ref[jnp.minimum(second, total - 1)]
            far = pltpu.roll(jnp.where(tile_lane >= shift, begin, rest), lax.rem(LANES - shift, LANES), 1)
            near = near_ref[jnp.maximum(first - total, 0)]
            send_ref[y, k] = jnp.where(first < total, far, near)


def final_kernel(recv_ref, rows_ref, live_ref, mass_ref, same_ref, other_ref, owned_ref, out_ref, gram_ref, slot_ref):
    snaps = mass_ref.shape[0]
    parts = []
    for k in range(4):
        live = live_ref[k : k + 1, :].astype(F32)
        parts.append(jnp.concatenate([recv_ref[y, k] for y in range(4)], axis=0) * live)
    fill_one_hot(slot_ref, [jnp.concatenate([rows_ref[k : k + 1, :] for k in range(4)], axis=1)])
    added = lax.dot_general(split2(jnp.concatenate(parts, axis=1)), slot_ref[...], NT, preferred_element_type=F32)
    total = mass_ref[...] + (added[:snaps] + added[snaps:])
    out_ref[...] = total
    total2 = split2(total)
    owned = owned_ref[...].astype(F32)
    core = lax.axis_index("core")
    here = lax.axis_index("x")
    for index, ref in ((core, same_ref), (1 - core, other_ref)):
        count = ref.shape[0]
        both = lax.dot_general(total2, split2(ref[...] * owned), NT, preferred_element_type=F32)
        terms = both[:snaps, :count] + (both[snaps:, :count] + both[:snaps, count:])
        for away in range(count // snaps):
            group = lax.rem(here + count // snaps - away, count // snaps)
            gram_ref[index, group] = terms[:, away * snaps : (away + 1) * snaps]


def gather_kernel(scale, recv_ref, out_ref):
    total = recv_ref[0]
    for z in range(1, recv_ref.shape[0]):
        total = total + recv_ref[z]
    total = total * scale
    groups, columns = total.shape[0], out_ref.shape[0]
    width = LANES // columns
    for c in range(columns):
        for half in range(groups // columns):
            out_ref[c : c + 1, half * LANES : (half + 1) * LANES] = jnp.concatenate(
                [total[half * columns + q : half * columns + q + 1, c * width : (c + 1) * width] for q in range(columns)],
                axis=1,
            )


def vmem(count):
    return [pl.BlockSpec(memory_space=pltpu.VMEM)] * count


SMEM = pl.BlockSpec(memory_space=pltpu.SMEM)
HBM = pl.BlockSpec(memory_space=pltpu.HBM)
ANY = pl.BlockSpec(memory_space=pl.ANY)


def route(recv, blocks, slots, zs):
    scratch = [pltpu.SMEM((16, LANES), jnp.int32), pltpu.SemaphoreType.DMA]
    send, table = pl.pallas_call(
        lambda *refs: spread_kernel(slots, *refs),
        out_shape=(jax.ShapeDtypeStruct((zs * slots, 8, LANES), F32), jax.ShapeDtypeStruct((16, LANES), jnp.int32)),
        in_specs=vmem(1),
        out_specs=tuple(vmem(2)),
        scratch_shapes=scratch,
        name="spread",
    )(recv)
    far = lax.all_to_all(send, "z", 0, 0, tiled=True)
    rows, nodes = blocks[0].shape
    return pl.pallas_call(
        lambda *refs: collect_kernel(slots, *refs),
        out_shape=(
            jax.ShapeDtypeStruct((4, 4, 8, LANES), F32),
            jax.ShapeDtypeStruct((1, 1), jnp.int32),
            jax.ShapeDtypeStruct((len(blocks) * rows, nodes), F32),
        ),
        in_specs=vmem(3 + len(blocks)),
        out_specs=tuple(vmem(3)),
        scratch_shapes=scratch,
        compiler_params=pltpu.CompilerParams(vmem_limit_bytes=20 * 1024 * 1024),
        name="collect",
    )(table, recv.reshape(20, 8, LANES), far, *blocks)


def per_device(snapshots, connect, elem_mask, volume, owned, peer_ids, peer_back, iface_rows, iface_mask):
    snaps, nodes = snapshots.shape
    zs, ys = lax.axis_size("z"), lax.axis_size("y")
    groups = lax.axis_size("x") * lax.axis_size("core")
    params = pltpu.CompilerParams(vmem_limit_bytes=40 * 1024 * 1024)
    xs, cores = lax.axis_size("x"), lax.axis_size("core")
    blocks = [snapshots]
    for away in range(1, xs):
        blocks.append(lax.ppermute(snapshots, "x", [(x, (x + away) % xs) for x in range(xs)]))
    given = (snapshots, connect, elem_mask[None], volume[None], iface_rows[0], iface_mask[0])
    mass, send = pl.pallas_call(
        local_kernel,
        out_shape=(jax.ShapeDtypeStruct((snaps, nodes), F32), jax.ShapeDtypeStruct((ys, 5, 8, LANES), F32)),
        in_specs=[SMEM, SMEM] + [ANY] * 6,
        out_specs=tuple(vmem(2)),
        scratch_shapes=[pltpu.VMEM(x.shape, x.dtype) for x in given]
        + [
            pltpu.VMEM((2, nodes, CHUNK), BF16),
            pltpu.VMEM((2, 2 * snaps + 16, CHUNK), BF16),
            pltpu.VMEM((2 * snaps + 16, nodes), F32),
            pltpu.VMEM((nodes, 4 * LANES), BF16),
            pltpu.SemaphoreType.DMA((6,)),
        ],
        compiler_params=pltpu.CompilerParams(vmem_limit_bytes=60 * 1024 * 1024),
        cost_estimate=pl.CostEstimate(flops=10**10, bytes_accessed=10**6, transcendentals=0),
        name="local_mass",
    )(peer_ids, peer_back, *given)
    recv = lax.all_to_all(send, "y", 0, 0, tiled=True)
    picked, short, snaps_x = route(recv, blocks, SLOTS, zs)
    snaps_other = lax.ppermute(snaps_x, "core", [(c, (c + 1) % cores) for c in range(cores)])
    picked = lax.cond(short[0, 0] > 0, lambda r, p: route(r, [r[0, 0]], 16, zs)[0], lambda r, p: p, recv, picked)
    recv = lax.all_to_all(picked, "y", 0, 0, tiled=True)
    mass_snap, gram = pl.pallas_call(
        final_kernel,
        out_shape=(
            jax.ShapeDtypeStruct((snaps, nodes), F32),
            jax.ShapeDtypeStruct((cores, xs, snaps, snaps), F32),
        ),
        in_specs=vmem(7),
        out_specs=tuple(vmem(2)),
        scratch_shapes=[pltpu.VMEM((nodes, 4 * LANES), BF16)],
        compiler_params=params,
        name="assemble_gram",
    )(recv, iface_rows[0], iface_mask[0], mass, snaps_x, snaps_other, owned[None])
    per_z = snaps // (ys * 4)
    gram = gram.reshape(cores, xs, per_z, ys, 4, snaps).transpose(3, 1, 0, 2, 4, 5)
    gram = lax.all_to_all(gram.reshape(ys * groups, per_z * 4 * snaps), ("y", "x", "core"), 0, 0, tiled=True)
    gram = jnp.sum(gram.reshape(ys, zs, 1, 4 * snaps), axis=0)
    gram = jnp.broadcast_to(gram, (zs, groups, 4 * snaps)).reshape(zs * groups, 4 * snaps)
    gram = lax.all_to_all(gram, ("z", "x", "core"), 0, 0, tiled=True)
    gram = pl.pallas_call(
        lambda *refs: gather_kernel(1.0 / (zs * ys * nodes), *refs),
        out_shape=jax.ShapeDtypeStruct((4, groups * snaps), F32),
        in_specs=vmem(1),
        out_specs=vmem(1)[0],
        name="sum_columns",
    )(gram.reshape(zs, groups, 4 * snaps))
    return mass_snap, gram.T


def solution(mesh):
    sizes = (16, 4, 4, 2)
    fine = Mesh(mesh.devices.reshape(sizes), ("z", "y", "x", "core"))
    part, snap = ("z", "y"), ("x", "core")
    in_specs = (
        P(snap, part),
        P(None, part),
        P(part),
        P(part),
        P(part),
        P(part, None),
        P(part, None),
        P(part, None, None),
        P(part, None, None),
    )
    out_specs = (P(snap, part), P(None, part))
    return jax.shard_map(per_device, mesh=fine, in_specs=in_specs, out_specs=out_specs, check_vma=False)
```

```python
import jax
import jax.numpy as jnp
from jax import lax
from jax.experimental import pallas as pl
from jax.experimental.pallas import tpu as pltpu
from jax.sharding import Mesh, PartitionSpec as P

F32 = jnp.float32
BF16 = jnp.bfloat16
NT = (((1,), (1,)), ((), ()))
CHUNK = 256
LANES = 128
SLOTS = 4
OVERFLOW = 1e30


def split2(x):
    high = x.astype(BF16)
    low = (x - high.astype(F32)).astype(BF16)
    return jnp.concatenate([high, low], axis=0)


def one_hot_block(lists, first, rows):
    iota = lax.broadcasted_iota(jnp.int32, (rows, lists[0].shape[1]), 0).astype(F32).astype(BF16)
    count = None
    for entry in lists:
        near = (entry - first).astype(F32).astype(BF16)
        hit = jnp.where(iota == near, jnp.ones((), BF16), jnp.zeros((), BF16))
        count = hit if count is None else count + hit
    return count


def fill_one_hot(ref, lists):
    for first in range(0, ref.shape[0], 256):
        ref[first : first + 256, :] = one_hot_block(lists, first, 256)


def local_kernel(*refs):
    far, (out_ref, send_ref), here = refs[:8], refs[8:10], refs[10:18]
    hot_ref, turned_ref, left_ref, acc_ref, slot_ref, mass_ref, sems = refs[18:]
    copies = [pltpu.make_async_copy(a, b, sems.at[i]) for i, (a, b) in enumerate(zip(far, here))]
    for copy in copies:
        copy.start()
    conn_ref, mask_ref, vol_ref, snap_ref, rows_ref, live_ref, peer_ref, back_ref = here
    snaps = snap_ref.shape[0]
    steps = conn_ref.shape[1] // CHUNK

    def fill(step):
        cols = slice(step * CHUNK, (step + 1) * CHUNK)
        lists = [conn_ref[i : i + 1, cols] for i in range(4)]
        for first in range(0, hot_ref.shape[1], 256):
            block = one_hot_block(lists, first, 256)
            hot_ref[step % 3, first : first + 256, :] = block
            turned_ref[step % 3, :, first : first + 256] = block.T

    def element(step):
        cols = slice(step * CHUNK, (step + 1) * CHUNK)
        weight = vol_ref[:, cols] * (mask_ref[:, cols].astype(F32) * 0.05)
        both = jnp.dot(snap2, hot_ref[step % 3], preferred_element_type=F32)
        value = (both[:snaps] + both[snaps:]) * weight
        left_ref[step % 3] = jnp.concatenate([split2(value), split2(jnp.broadcast_to(weight, (8, CHUNK)))], axis=0)

    def add(step):
        part = jnp.dot(left_ref[step % 3], turned_ref[step % 3], preferred_element_type=F32)
        acc_ref[...] = part if step == 0 else acc_ref[...] + part

    copies[0].wait()
    fill(0)
    for copy in copies[1:]:
        copy.wait()
    snap = snap_ref[...]
    snap2 = split2(snap)
    fill_one_hot(slot_ref, [jnp.concatenate([rows_ref[k : k + 1, :] for k in range(4)], axis=1)])
    fill(1)
    for step in range(steps):
        element(step)
        if step > 0:
            add(step - 1)
        if step + 2 < steps:
            fill(step + 2)
    add(steps - 1)
    diag = acc_ref[2 * snaps : 2 * snaps + 1] + acc_ref[2 * snaps + 8 : 2 * snaps + 9]
    mass = acc_ref[:snaps] + acc_ref[snaps : 2 * snaps] + snap * diag
    mass_ref[...] = mass
    copy = pltpu.make_async_copy(mass_ref, out_ref, sems.at[8])
    copy.start()
    both = jnp.dot(split2(mass), slot_ref[...], preferred_element_type=F32)
    picked = both[:snaps] + both[snaps:]
    used = jnp.sum(live_ref[...].astype(F32), axis=1, keepdims=True)
    for carrier in range(4):
        for k in range(4):
            send_ref[carrier, k] = picked[carrier * 8 : carrier * 8 + 8, k * LANES : (k + 1) * LANES]
            whence = jnp.full((1, LANES), peer_ref[0, k] * 4 + back_ref[0, k], jnp.int32)
            send_ref[carrier, 4, k : k + 1] = whence.astype(F32)
        send_ref[carrier, 4, 4:8] = jnp.broadcast_to(used, (4, LANES))
    copy.wait()


def to_row(column, inside):
    return jnp.sum(jnp.where(inside, column, 0), axis=0, keepdims=True)


def pack(first, second, shift):
    return second * (1 << 19) + first * (1 << 7) + shift


def unpack(word):
    return (word >> 7) & 4095, word >> 19, word & 127


def spread_kernel(slots, recv_ref, send_ref, table_ref):
    me = lax.axis_index("z")
    whence = jnp.concatenate([recv_ref[y, 4, 0:4] for y in range(4)], axis=0).astype(jnp.int32)
    used = jnp.concatenate([recv_ref[y, 4, 4:8] for y in range(4)], axis=0).astype(jnp.int32)
    lane = lax.broadcasted_iota(jnp.int32, (16, LANES), 1)
    sub = lax.broadcasted_iota(jnp.int32, (16, LANES), 0)
    line = whence // 16
    key = whence % 16
    same = (line == to_row(line, lane == sub)) & (lane < 16)
    width = to_row(used, lane == sub)
    sent = jnp.sum(jnp.where(same & (lane < sub), width, 0), axis=1, keepdims=True)
    came = jnp.sum(jnp.where(same & (to_row(key, lane == sub) < key), width, 0), axis=1, keepdims=True)
    home = line == me
    sent = jnp.where(home, 0, sent)
    total = send_ref.shape[0]
    last = line * slots + slots - 1
    there = line * slots + jnp.minimum(sent // LANES, slots - 1)
    here = line * slots + jnp.minimum(came // LANES, slots - 1)
    near = total + (key // 4) * 5 + key % 4
    table_ref[...] = jnp.broadcast_to(
        jnp.where(home, near * ((1 << 19) + (1 << 7)), pack(here, jnp.minimum(here + 1, last), came % LANES)), (16, LANES)
    )
    word = pack(there, jnp.minimum(there + 1, last), sent % LANES)
    send_ref[...] = jnp.zeros_like(send_ref)
    over = jnp.max(jnp.where(home, 0, sent + used - slots * LANES), axis=0, keepdims=True)[:, 0:1] > 0
    tile_lane = lax.broadcasted_iota(jnp.int32, (8, LANES), 1)
    for y in range(4):
        for k in range(4):
            e = y * 4 + k
            first, second, shift = unpack(word[e, 0])
            live = tile_lane < recv_ref[y, 4, 4 + k : 5 + k].astype(jnp.int32)
            moved = pltpu.roll(jnp.where(live, recv_ref[y, k], 0.0), shift, 1)
            send_ref[first] = send_ref[first] + jnp.where(tile_lane >= shift, moved, 0.0)
            send_ref[second] = send_ref[second] + jnp.where(tile_lane < shift, moved, 0.0)
    for z in range(zs_of(send_ref, slots)):
        send_ref[z * slots] = jnp.where(over, OVERFLOW, send_ref[z * slots])


def zs_of(ref, slots):
    return ref.shape[0] // slots


def collect_kernel(slots, table_ref, near_ref, far_ref, owned_ref, rows_ref, live_ref, *refs):
    *blocks, send_ref, flag_ref, all_ref, count_ref, list_ref, used_ref = refs
    table = table_ref[...]
    top = far_ref[0]
    for z in range(1, zs_of(far_ref, slots)):
        top = jnp.maximum(top, far_ref[z * slots])
    flag_ref[...] = jnp.where(top[0:1, 0:1] > OVERFLOW * 0.5, 1, 0)
    count_ref[...] = owned_ref[...].astype(F32)
    list_ref[...] = rows_ref[...]
    used_ref[...] = live_ref[...].astype(F32)
    for index, block in enumerate(blocks):
        rows = block.shape[0]
        all_ref[index * rows : (index + 1) * rows] = block[...]
    total = far_ref.shape[0]
    tile_lane = lax.broadcasted_iota(jnp.int32, (8, LANES), 1)
    for y in range(4):
        for k in range(4):
            e = y * 4 + k
            first, second, shift = unpack(table[e, 0])
            begin, rest = far_ref[jnp.minimum(first, total - 1)], far_ref[jnp.minimum(second, total - 1)]
            far = pltpu.roll(jnp.where(tile_lane >= shift, begin, rest), lax.rem(LANES - shift, LANES), 1)
            near = near_ref[jnp.maximum(first - total, 0)]
            send_ref[y, k] = jnp.where(first < total, far, near)


def final_kernel(recv_ref, rows_ref, live_ref, mass_ref, same_ref, other_ref, owned_ref, out_ref, gram_ref, slot_ref):
    snaps = mass_ref.shape[0]
    parts = []
    for k in range(4):
        live = live_ref[k : k + 1, :]
        parts.append(jnp.concatenate([recv_ref[y, k] for y in range(4)], axis=0) * live)
    fill_one_hot(slot_ref, [jnp.concatenate([rows_ref[k : k + 1, :] for k in range(4)], axis=1)])
    added = lax.dot_general(split2(jnp.concatenate(parts, axis=1)), slot_ref[...], NT, preferred_element_type=F32)
    total = mass_ref[...] + (added[:snaps] + added[snaps:])
    out_ref[...] = total
    total2 = split2(total)
    owned = owned_ref[...]
    core = lax.axis_index("core")
    here = lax.axis_index("x")
    for index, ref in ((core, same_ref), (1 - core, other_ref)):
        count = ref.shape[0]
        both = lax.dot_general(total2, split2(ref[...] * owned), NT, preferred_element_type=F32)
        terms = both[:snaps, :count] + (both[snaps:, :count] + both[:snaps, count:])
        for away in range(count // snaps):
            group = lax.rem(here + count // snaps - away, count // snaps)
            gram_ref[index, group] = terms[:, away * snaps : (away + 1) * snaps]


def gather_kernel(scale, recv_ref, out_ref):
    total = recv_ref[0]
    for z in range(1, recv_ref.shape[0]):
        total = total + recv_ref[z]
    total = total * scale
    groups, columns = total.shape[0], out_ref.shape[0]
    width = LANES // columns
    block = lax.broadcasted_iota(jnp.int32, (groups, LANES), 1) // width
    place = lax.broadcasted_iota(jnp.int32, (groups, LANES), 0) % columns
    out = jnp.zeros((groups, LANES), F32)
    for away in range(columns):
        turned = total if away == 0 else pltpu.roll(total, away * width, 1)
        turned = jnp.where(block == place, turned, 0.0)
        if away > 0:
            near = pltpu.roll(turned, groups - away, 0)
            wrapped = pltpu.roll(turned, (groups - away + columns) % groups, 0)
            turned = jnp.where(place + away < columns, near, wrapped)
        out = out + turned
    for half in range(groups // columns):
        out_ref[:, half * LANES : (half + 1) * LANES] = out[half * columns : (half + 1) * columns]


def vmem(count):
    return [pl.BlockSpec(memory_space=pltpu.VMEM)] * count


ANY = pl.BlockSpec(memory_space=pl.ANY)
SMALL = pltpu.CompilerParams(vmem_limit_bytes=20 * 1024 * 1024)


def route(recv, blocks, owned, lists, live, slots, zs):
    send, table = pl.pallas_call(
        lambda *refs: spread_kernel(slots, *refs),
        out_shape=(jax.ShapeDtypeStruct((zs * slots, 8, LANES), F32), jax.ShapeDtypeStruct((16, LANES), jnp.int32)),
        in_specs=vmem(1),
        out_specs=tuple(vmem(2)),
        compiler_params=SMALL,
        name="spread",
    )(recv)
    far = lax.all_to_all(send, "z", 0, 0, tiled=True)
    rows, nodes = blocks[0].shape
    return pl.pallas_call(
        lambda *refs: collect_kernel(slots, *refs),
        out_shape=(
            jax.ShapeDtypeStruct((4, 4, 8, LANES), F32),
            jax.ShapeDtypeStruct((1, 1), jnp.int32),
            jax.ShapeDtypeStruct((len(blocks) * rows, nodes), F32),
            jax.ShapeDtypeStruct(owned.shape, F32),
            jax.ShapeDtypeStruct(lists.shape, jnp.int32),
            jax.ShapeDtypeStruct(live.shape, F32),
        ),
        in_specs=vmem(6 + len(blocks)),
        out_specs=tuple(vmem(6)),
        compiler_params=SMALL,
        name="collect",
    )(table, recv.reshape(20, 8, LANES), far, owned, lists, live, *blocks)


def per_device(snapshots, connect, elem_mask, volume, owned, peer_ids, peer_back, iface_rows, iface_mask):
    snaps, nodes = snapshots.shape
    zs, ys = lax.axis_size("z"), lax.axis_size("y")
    groups = lax.axis_size("x") * lax.axis_size("core")
    params = pltpu.CompilerParams(vmem_limit_bytes=40 * 1024 * 1024)
    xs, cores = lax.axis_size("x"), lax.axis_size("core")
    blocks = [snapshots]
    for away in range(1, xs):
        blocks.append(lax.ppermute(snapshots, "x", [(x, (x + away) % xs) for x in range(xs)]))
    given = (connect, elem_mask[None], volume[None], snapshots, iface_rows[0], iface_mask[0])
    room = [pltpu.VMEM(x.shape, x.dtype) for x in given] + [pltpu.SMEM(peer_ids.shape, jnp.int32)] * 2
    mass, send = pl.pallas_call(
        local_kernel,
        out_shape=(jax.ShapeDtypeStruct((snaps, nodes), F32), jax.ShapeDtypeStruct((ys, 5, 8, LANES), F32)),
        in_specs=[ANY] * 8,
        out_specs=(ANY, vmem(1)[0]),
        scratch_shapes=room
        + [
            pltpu.VMEM((3, nodes, CHUNK), BF16),
            pltpu.VMEM((3, CHUNK, nodes), BF16),
            pltpu.VMEM((3, 2 * snaps + 16, CHUNK), BF16),
            pltpu.VMEM((2 * snaps + 16, nodes), F32),
            pltpu.VMEM((nodes, 4 * LANES), BF16),
            pltpu.VMEM((snaps, nodes), F32),
            pltpu.SemaphoreType.DMA((9,)),
        ],
        compiler_params=pltpu.CompilerParams(vmem_limit_bytes=60 * 1024 * 1024),
        cost_estimate=pl.CostEstimate(flops=10**10, bytes_accessed=10**6, transcendentals=0),
        name="local_mass",
    )(*given, peer_ids, peer_back)
    recv = lax.all_to_all(send, "y", 0, 0, tiled=True)
    picked, short, snaps_x, counted, lists, live = route(
        recv, blocks, owned[None], iface_rows[0], iface_mask[0], SLOTS, zs
    )
    none = jnp.zeros((4, LANES), jnp.int32)
    snaps_other = lax.ppermute(snaps_x, "core", [(c, (c + 1) % cores) for c in range(cores)])
    picked = lax.cond(short[0, 0] > 0, lambda r, p: route(r, [r[0, 0]], none, none, none, 16, zs)[0], lambda r, p: p, recv, picked)
    recv = lax.all_to_all(picked, "y", 0, 0, tiled=True)
    mass_snap, gram = pl.pallas_call(
        final_kernel,
        out_shape=(
            jax.ShapeDtypeStruct((snaps, nodes), F32),
            jax.ShapeDtypeStruct((cores, xs, snaps, snaps), F32),
        ),
        in_specs=vmem(7),
        out_specs=tuple(vmem(2)),
        scratch_shapes=[pltpu.VMEM((nodes, 4 * LANES), BF16)],
        compiler_params=params,
        name="assemble_gram",
    )(recv, lists, live, mass, snaps_x, snaps_other, counted)
    per_z = snaps // (ys * 4)
    gram = gram.reshape(cores, xs, per_z, ys, 4, snaps).transpose(3, 1, 0, 2, 4, 5)
    gram = lax.all_to_all(gram.reshape(ys * groups, per_z * 4 * snaps), ("y", "x", "core"), 0, 0, tiled=True)
    gram = jnp.sum(gram.reshape(ys, zs, 1, 4 * snaps), axis=0)
    gram = jnp.broadcast_to(gram, (zs, groups, 4 * snaps)).reshape(zs * groups, 4 * snaps)
    gram = lax.all_to_all(gram, ("z", "x", "core"), 0, 0, tiled=True)
    gram = pl.pallas_call(
        lambda *refs: gather_kernel(1.0 / (zs * ys * nodes), *refs),
        out_shape=jax.ShapeDtypeStruct((4, groups * snaps), F32),
        in_specs=vmem(1),
        out_specs=vmem(1)[0],
        compiler_params=SMALL,
        name="sum_columns",
    )(gram.reshape(zs, groups, 4 * snaps))
    return mass_snap, gram.T


def solution(mesh):
    sizes = (16, 4, 4, 2)
    fine = Mesh(mesh.devices.reshape(sizes), ("z", "y", "x", "core"))
    part, snap = ("z", "y"), ("x", "core")
    in_specs = (
        P(snap, part),
        P(None, part),
        P(part),
        P(part),
        P(part),
        P(part, None),
        P(part, None),
        P(part, None, None),
        P(part, None, None),
    )
    out_specs = (P(snap, part), P(None, part))
    return jax.shard_map(per_device, mesh=fine, in_specs=in_specs, out_specs=out_specs, check_vma=False)
```

```python
import jax
import jax.numpy as jnp
from jax import lax
from jax.experimental import pallas as pl
from jax.experimental.pallas import tpu as pltpu
from jax.sharding import Mesh, PartitionSpec as P

F32 = jnp.float32
BF16 = jnp.bfloat16
NT = (((1,), (1,)), ((), ()))
CHUNK = 256
LANES = 128
SLOTS = 4
OVERFLOW = 1e30


def split2(x):
    high = x.astype(BF16)
    low = (x - high.astype(F32)).astype(BF16)
    return jnp.concatenate([high, low], axis=0)


def one_hot_block(lists, first, rows):
    iota = lax.broadcasted_iota(jnp.int32, (rows, lists[0].shape[1]), 0).astype(F32).astype(BF16)
    count = None
    for entry in lists:
        near = (entry - first).astype(F32).astype(BF16)
        hit = jnp.where(iota == near, jnp.ones((), BF16), jnp.zeros((), BF16))
        count = hit if count is None else count + hit
    return count


def fill_one_hot(ref, lists):
    for first in range(0, ref.shape[0], 256):
        ref[first : first + 256, :] = one_hot_block(lists, first, 256)


def local_kernel(*refs):
    far, (out_ref, send_ref), here = refs[:8], refs[8:10], refs[10:18]
    hot_ref, turned_ref, left_ref, acc_ref, slot_ref, mass_ref, sems = refs[18:]
    copies = [pltpu.make_async_copy(a, b, sems.at[i]) for i, (a, b) in enumerate(zip(far, here))]
    for copy in copies:
        copy.start()
    conn_ref, mask_ref, vol_ref, snap_ref, rows_ref, live_ref, peer_ref, back_ref = here
    snaps = snap_ref.shape[0]
    steps = conn_ref.shape[1] // CHUNK

    def fill(step):
        cols = slice(step * CHUNK, (step + 1) * CHUNK)
        lists = [conn_ref[i : i + 1, cols] for i in range(4)]
        for first in range(0, hot_ref.shape[1], 256):
            block = one_hot_block(lists, first, 256)
            hot_ref[step % 3, first : first + 256, :] = block
            turned_ref[step % 3, :, first : first + 256] = block.T

    def element(step):
        cols = slice(step * CHUNK, (step + 1) * CHUNK)
        weight = vol_ref[:, cols] * (mask_ref[:, cols].astype(F32) * 0.05)
        both = jnp.dot(snap2, hot_ref[step % 3], preferred_element_type=F32)
        value = (both[:snaps] + both[snaps:]) * weight
        left_ref[step % 3] = jnp.concatenate([split2(value), split2(jnp.broadcast_to(weight, (8, CHUNK)))], axis=0)

    def add(step):
        part = jnp.dot(left_ref[step % 3], turned_ref[step % 3], preferred_element_type=F32)
        acc_ref[...] = part if step == 0 else acc_ref[...] + part

    copies[0].wait()
    fill(0)
    fill(1)
    for copy in copies[1:4]:
        copy.wait()
    snap = snap_ref[...]
    snap2 = split2(snap)
    for step in range(steps):
        element(step)
        if step > 0:
            add(step - 1)
        if step + 2 < steps:
            fill(step + 2)
    for copy in copies[4:]:
        copy.wait()
    fill_one_hot(slot_ref, [jnp.concatenate([rows_ref[k : k + 1, :] for k in range(4)], axis=1)])
    add(steps - 1)
    diag = acc_ref[2 * snaps : 2 * snaps + 1] + acc_ref[2 * snaps + 8 : 2 * snaps + 9]
    mass = acc_ref[:snaps] + acc_ref[snaps : 2 * snaps] + snap * diag
    mass_ref[...] = mass
    copy = pltpu.make_async_copy(mass_ref, out_ref, sems.at[8])
    copy.start()
    both = jnp.dot(split2(mass), slot_ref[...], preferred_element_type=F32)
    picked = both[:snaps] + both[snaps:]
    used = jnp.sum(live_ref[...].astype(F32), axis=1, keepdims=True)
    for carrier in range(4):
        for k in range(4):
            send_ref[carrier, k] = picked[carrier * 8 : carrier * 8 + 8, k * LANES : (k + 1) * LANES]
            whence = jnp.full((1, LANES), peer_ref[0, k] * 4 + back_ref[0, k], jnp.int32)
            send_ref[carrier, 4, k : k + 1] = whence.astype(F32)
        send_ref[carrier, 4, 4:8] = jnp.broadcast_to(used, (4, LANES))
    copy.wait()


def to_row(column, inside):
    return jnp.sum(jnp.where(inside, column, 0), axis=0, keepdims=True)


def pack(first, second, shift):
    return second * (1 << 19) + first * (1 << 7) + shift


def unpack(word):
    return (word >> 7) & 4095, word >> 19, word & 127


def spread_kernel(slots, recv_ref, send_ref, table_ref):
    me = lax.axis_index("z")
    whence = jnp.concatenate([recv_ref[y, 4, 0:4] for y in range(4)], axis=0).astype(jnp.int32)
    used = jnp.concatenate([recv_ref[y, 4, 4:8] for y in range(4)], axis=0).astype(jnp.int32)
    lane = lax.broadcasted_iota(jnp.int32, (16, LANES), 1)
    sub = lax.broadcasted_iota(jnp.int32, (16, LANES), 0)
    line = whence // 16
    key = whence % 16
    same = (line == to_row(line, lane == sub)) & (lane < 16)
    width = to_row(used, lane == sub)
    sent = jnp.sum(jnp.where(same & (lane < sub), width, 0), axis=1, keepdims=True)
    came = jnp.sum(jnp.where(same & (to_row(key, lane == sub) < key), width, 0), axis=1, keepdims=True)
    home = line == me
    sent = jnp.where(home, 0, sent)
    total = send_ref.shape[0]
    last = line * slots + slots - 1
    there = line * slots + jnp.minimum(sent // LANES, slots - 1)
    here = line * slots + jnp.minimum(came // LANES, slots - 1)
    near = total + (key // 4) * 5 + key % 4
    table_ref[...] = jnp.broadcast_to(
        jnp.where(home, near * ((1 << 19) + (1 << 7)), pack(here, jnp.minimum(here + 1, last), came % LANES)), (16, LANES)
    )
    word = pack(there, jnp.minimum(there + 1, last), sent % LANES)
    send_ref[...] = jnp.zeros_like(send_ref)
    over = jnp.max(jnp.where(home, 0, sent + used - slots * LANES), axis=0, keepdims=True)[:, 0:1] > 0
    tile_lane = lax.broadcasted_iota(jnp.int32, (8, LANES), 1)
    for y in range(4):
        for k in range(4):
            e = y * 4 + k
            first, second, shift = unpack(word[e, 0])
            live = tile_lane < recv_ref[y, 4, 4 + k : 5 + k].astype(jnp.int32)
            moved = pltpu.roll(jnp.where(live, recv_ref[y, k], 0.0), shift, 1)
            send_ref[first] = send_ref[first] + jnp.where(tile_lane >= shift, moved, 0.0)
            send_ref[second] = send_ref[second] + jnp.where(tile_lane < shift, moved, 0.0)
    for z in range(zs_of(send_ref, slots)):
        send_ref[z * slots] = jnp.where(over, OVERFLOW, send_ref[z * slots])


def zs_of(ref, slots):
    return ref.shape[0] // slots


def collect_kernel(slots, table_ref, near_ref, far_ref, owned_ref, rows_ref, live_ref, *refs):
    *blocks, send_ref, flag_ref, all_ref, count_ref, list_ref, used_ref = refs
    table = table_ref[...]
    top = far_ref[0]
    for z in range(1, zs_of(far_ref, slots)):
        top = jnp.maximum(top, far_ref[z * slots])
    flag_ref[...] = jnp.where(top[0:1, 0:1] > OVERFLOW * 0.5, 1, 0)
    count_ref[...] = owned_ref[...].astype(F32)
    list_ref[...] = rows_ref[...]
    used_ref[...] = live_ref[...].astype(F32)
    for index, block in enumerate(blocks):
        rows = block.shape[0]
        all_ref[index * rows : (index + 1) * rows] = block[...]
    total = far_ref.shape[0]
    tile_lane = lax.broadcasted_iota(jnp.int32, (8, LANES), 1)
    for y in range(4):
        for k in range(4):
            e = y * 4 + k
            first, second, shift = unpack(table[e, 0])
            begin, rest = far_ref[jnp.minimum(first, total - 1)], far_ref[jnp.minimum(second, total - 1)]
            far = pltpu.roll(jnp.where(tile_lane >= shift, begin, rest), lax.rem(LANES - shift, LANES), 1)
            near = near_ref[jnp.maximum(first - total, 0)]
            send_ref[y, k] = jnp.where(first < total, far, near)


def final_kernel(recv_ref, rows_ref, live_ref, mass_ref, same_ref, other_ref, owned_ref, out_ref, gram_ref, slot_ref):
    snaps = mass_ref.shape[0]
    parts = []
    for k in range(4):
        live = live_ref[k : k + 1, :]
        parts.append(jnp.concatenate([recv_ref[y, k] for y in range(4)], axis=0) * live)
    fill_one_hot(slot_ref, [jnp.concatenate([rows_ref[k : k + 1, :] for k in range(4)], axis=1)])
    added = lax.dot_general(split2(jnp.concatenate(parts, axis=1)), slot_ref[...], NT, preferred_element_type=F32)
    total = mass_ref[...] + (added[:snaps] + added[snaps:])
    out_ref[...] = total
    total2 = split2(total)
    owned = owned_ref[...]
    core = lax.axis_index("core")
    here = lax.axis_index("x")
    for index, ref in ((core, same_ref), (1 - core, other_ref)):
        count = ref.shape[0]
        both = lax.dot_general(total2, split2(ref[...] * owned), NT, preferred_element_type=F32)
        terms = both[:snaps, :count] + (both[snaps:, :count] + both[:snaps, count:])
        for away in range(count // snaps):
            group = lax.rem(here + count // snaps - away, count // snaps)
            gram_ref[index, group] = terms[:, away * snaps : (away + 1) * snaps]


def gather_kernel(scale, recv_ref, out_ref):
    total = recv_ref[0]
    for z in range(1, recv_ref.shape[0]):
        total = total + recv_ref[z]
    total = total * scale
    groups, columns = total.shape[0], out_ref.shape[0]
    width = LANES // columns
    block = lax.broadcasted_iota(jnp.int32, (groups, LANES), 1) // width
    place = lax.broadcasted_iota(jnp.int32, (groups, LANES), 0) % columns
    out = jnp.zeros((groups, LANES), F32)
    for away in range(columns):
        turned = total if away == 0 else pltpu.roll(total, away * width, 1)
        turned = jnp.where(block == place, turned, 0.0)
        if away > 0:
            near = pltpu.roll(turned, groups - away, 0)
            wrapped = pltpu.roll(turned, (groups - away + columns) % groups, 0)
            turned = jnp.where(place + away < columns, near, wrapped)
        out = out + turned
    for half in range(groups // columns):
        out_ref[:, half * LANES : (half + 1) * LANES] = out[half * columns : (half + 1) * columns]


def vmem(count):
    return [pl.BlockSpec(memory_space=pltpu.VMEM)] * count


ANY = pl.BlockSpec(memory_space=pl.ANY)
SMALL = pltpu.CompilerParams(vmem_limit_bytes=20 * 1024 * 1024)


def route(recv, blocks, owned, lists, live, slots, zs):
    send, table = pl.pallas_call(
        lambda *refs: spread_kernel(slots, *refs),
        out_shape=(jax.ShapeDtypeStruct((zs * slots, 8, LANES), F32), jax.ShapeDtypeStruct((16, LANES), jnp.int32)),
        in_specs=vmem(1),
        out_specs=tuple(vmem(2)),
        compiler_params=SMALL,
        name="spread",
    )(recv)
    far = lax.all_to_all(send, "z", 0, 0, tiled=True)
    rows, nodes = blocks[0].shape
    return pl.pallas_call(
        lambda *refs: collect_kernel(slots, *refs),
        out_shape=(
            jax.ShapeDtypeStruct((4, 4, 8, LANES), F32),
            jax.ShapeDtypeStruct((1, 1), jnp.int32),
            jax.ShapeDtypeStruct((len(blocks) * rows, nodes), F32),
            jax.ShapeDtypeStruct(owned.shape, F32),
            jax.ShapeDtypeStruct(lists.shape, jnp.int32),
            jax.ShapeDtypeStruct(live.shape, F32),
        ),
        in_specs=vmem(6 + len(blocks)),
        out_specs=tuple(vmem(6)),
        compiler_params=SMALL,
        name="collect",
    )(table, recv.reshape(20, 8, LANES), far, owned, lists, live, *blocks)


def per_device(snapshots, connect, elem_mask, volume, owned, peer_ids, peer_back, iface_rows, iface_mask):
    snaps, nodes = snapshots.shape
    zs, ys = lax.axis_size("z"), lax.axis_size("y")
    groups = lax.axis_size("x") * lax.axis_size("core")
    params = pltpu.CompilerParams(vmem_limit_bytes=40 * 1024 * 1024)
    xs, cores = lax.axis_size("x"), lax.axis_size("core")
    blocks = [snapshots]
    for away in range(1, xs):
        blocks.append(lax.ppermute(snapshots, "x", [(x, (x + away) % xs) for x in range(xs)]))
    given = (connect, elem_mask[None], volume[None], snapshots, iface_rows[0], iface_mask[0])
    room = [pltpu.VMEM(x.shape, x.dtype) for x in given] + [pltpu.SMEM(peer_ids.shape, jnp.int32)] * 2
    mass, send = pl.pallas_call(
        local_kernel,
        out_shape=(jax.ShapeDtypeStruct((snaps, nodes), F32), jax.ShapeDtypeStruct((ys, 5, 8, LANES), F32)),
        in_specs=[ANY] * 8,
        out_specs=(ANY, vmem(1)[0]),
        scratch_shapes=room
        + [
            pltpu.VMEM((3, nodes, CHUNK), BF16),
            pltpu.VMEM((3, CHUNK, nodes), BF16),
            pltpu.VMEM((3, 2 * snaps + 16, CHUNK), BF16),
            pltpu.VMEM((2 * snaps + 16, nodes), F32),
            pltpu.VMEM((nodes, 4 * LANES), BF16),
            pltpu.VMEM((snaps, nodes), F32),
            pltpu.SemaphoreType.DMA((9,)),
        ],
        compiler_params=pltpu.CompilerParams(vmem_limit_bytes=60 * 1024 * 1024),
        cost_estimate=pl.CostEstimate(flops=10**10, bytes_accessed=10**6, transcendentals=0),
        name="local_mass",
    )(*given, peer_ids, peer_back)
    recv = lax.all_to_all(send, "y", 0, 0, tiled=True)
    picked, short, snaps_x, counted, lists, live = route(
        recv, blocks, owned[None], iface_rows[0], iface_mask[0], SLOTS, zs
    )
    none = jnp.zeros((4, LANES), jnp.int32)
    snaps_other = lax.ppermute(snaps_x, "core", [(c, (c + 1) % cores) for c in range(cores)])
    picked = lax.cond(short[0, 0] > 0, lambda r, p: route(r, [r[0, 0]], none, none, none, 16, zs)[0], lambda r, p: p, recv, picked)
    recv = lax.all_to_all(picked, "y", 0, 0, tiled=True)
    mass_snap, gram = pl.pallas_call(
        final_kernel,
        out_shape=(
            jax.ShapeDtypeStruct((snaps, nodes), F32),
            jax.ShapeDtypeStruct((cores, xs, snaps, snaps), F32),
        ),
        in_specs=vmem(7),
        out_specs=tuple(vmem(2)),
        scratch_shapes=[pltpu.VMEM((nodes, 4 * LANES), BF16)],
        compiler_params=params,
        name="assemble_gram",
    )(recv, lists, live, mass, snaps_x, snaps_other, counted)
    per_z = snaps // (ys * 4)
    gram = gram.reshape(cores, xs, per_z, ys, 4, snaps).transpose(3, 1, 0, 2, 4, 5)
    gram = lax.all_to_all(gram.reshape(ys * groups, per_z * 4 * snaps), ("y", "x", "core"), 0, 0, tiled=True)
    gram = jnp.sum(gram.reshape(ys, zs, 1, 4 * snaps), axis=0)
    gram = jnp.broadcast_to(gram, (zs, groups, 4 * snaps)).reshape(zs * groups, 4 * snaps)
    gram = lax.all_to_all(gram, ("z", "x", "core"), 0, 0, tiled=True)
    gram = pl.pallas_call(
        lambda *refs: gather_kernel(1.0 / (zs * ys * nodes), *refs),
        out_shape=jax.ShapeDtypeStruct((4, groups * snaps), F32),
        in_specs=vmem(1),
        out_specs=vmem(1)[0],
        compiler_params=SMALL,
        name="sum_columns",
    )(gram.reshape(zs, groups, 4 * snaps))
    return mass_snap, gram.T


def solution(mesh):
    sizes = (16, 4, 4, 2)
    fine = Mesh(mesh.devices.reshape(sizes), ("z", "y", "x", "core"))
    part, snap = ("z", "y"), ("x", "core")
    in_specs = (
        P(snap, part),
        P(None, part),
        P(part),
        P(part),
        P(part),
        P(part, None),
        P(part, None),
        P(part, None, None),
        P(part, None, None),
    )
    out_specs = (P(snap, part), P(None, part))
    return jax.shard_map(per_device, mesh=fine, in_specs=in_specs, out_specs=out_specs, check_vma=False)
```
